256 devices in a mesh: seq: 8 (over x, core), expert: 32 (over z, y).
Axes of the slice: x: 4, y: 4, z: 8, core: 2. Of those that a mesh axis runs over, the one named last changes fastest.
Arguments:
- tokens: bfloat16 [8192, 2048], P('expert'), may hold values from -6 to 6
- routes: int32 [8192, 6], P('expert'), may hold values from 0 to 63, all different within a row; in each aligned block of 256 rows (0 to 255, 256 to 511, ...) at most 32 rows name the same one
- gates: float32 [8192, 6], P('expert'), may hold values from 0.05 to 0.5
- expert_gate: bfloat16 [64, 2048, 1408], P('expert', None, 'seq'), may hold values from -0.125 to 0.125
- expert_up: bfloat16 [64, 2048, 1408], P('expert', None, 'seq'), may hold values from -0.125 to 0.125
- expert_down: bfloat16 [64, 1408, 2048], P('expert', 'seq'), may hold values from -0.15625 to 0.15625
- shared_gate: bfloat16 [2048, 2816], P(None, 'seq'), may hold values from -0.125 to 0.125
- shared_up: bfloat16 [2048, 2816], P(None, 'seq'), may hold values from -0.125 to 0.125
- shared_down: bfloat16 [2816, 2048], P('seq'), may hold values from -0.109375 to 0.109375
Outputs:
- mixed: bfloat16 [8192, 2048], P('expert', 'seq')
The draws below stay inside these ranges and needn't reach their ends.
Inputs may be any that keep to these rules, and one draw needn't show every extreme that they name: `routes`: in each aligned block of 256 rows no expert is named by more than 32 rows, a bound that some block reaches; the numbers in one row differ.
All inputs are finite; a program needn't handle non-finite values.
Results may differ from the reference program's by a relative error of at most 0.02.
Values may be sent and summed in bfloat16 or wider, within the bound.
A program may use at most 128 MiB of HBM per device.

```python
import math
import jax
import jax.numpy as jnp
import numpy as np
from jax import lax

D = 2048
FF = 1408
TOP = 6
TOK_DEV = 256
EXPERTS = 64
SHARED_FF = 2816
CAP = 32
TOKENS = 8192
N_SEQ = 8


def block_scale(own_key, shape, pieces, least, high):
    level, own = 1.0, jax.random.fold_in(own_key, 6)
    for dim, shards_of in pieces:
        heights = jnp.exp(jax.random.uniform(jax.random.fold_in(own, dim), (shards_of,), jnp.float32, least / len(pieces), high / len(pieces)))
        level = level * jnp.repeat(heights, shape[dim] // shards_of).reshape([-1 if axis == dim else 1 for axis in range(len(shape))])
    return level


def assign_block(rng, own, number, rows, amount, top, reach, slope):
    ranking = jax.random.permutation(rng, amount)
    crowded, common = portions_of(amount, rows * top, reach, slope, True), portions_of(amount, rows * top, reach, slope, False)
    places = jnp.arange(amount)

    def named(sizes, rotation):
        used = int((sizes > 0).sum())
        fixed = max(1, used // 4)
        shifted = fixed + (places - fixed + rotation * (used - fixed)) % max(1, amount - fixed)
        return jnp.zeros((amount,), jnp.int32).at[ranking[jnp.where(places < fixed, places, shifted)]].set(jnp.asarray(sizes, jnp.int32))

    sizes = jnp.where(number % 4 == 0, named(crowded, number // 4), named(common, number - number // 4 - 1))
    mixed = jax.random.permutation(jax.random.fold_in(own, 3), amount)
    donor, receiver = mixed[0:amount // 2 * 2:2], mixed[1:amount // 2 * 2:2]
    margin = jnp.minimum(sizes[donor] - 1, reach - sizes[receiver]) // 2
    margin = jnp.where((donor == ranking[0]) | (receiver == ranking[0]) | (sizes[receiver] == 0), 0, jnp.maximum(margin, 0))
    shifted = jax.random.randint(jax.random.fold_in(own, 4), (amount // 2,), 0, 1 << 20) % (margin + 1)
    sizes = sizes.at[donor].add(-shifted).at[receiver].add(shifted)
    items = jnp.searchsorted(jnp.cumsum(sizes), jnp.arange(rows * top), side="right").astype(jnp.int32)
    table = items.reshape(top, rows).T
    table = table[jax.random.permutation(jax.random.fold_in(own, 1), rows)]
    rotation = jax.random.randint(jax.random.fold_in(own, 2), (rows, 1), 0, top)
    return jnp.take_along_axis(table, (jnp.arange(top)[None, :] + rotation) % top, axis=1)


def portions_of(amount, total, most, lean, full):
    loads = [(1 << 20) // math.isqrt(rank ** lean) + 1 for rank in range(1, amount + 1)]
    largest = most if full else min(most, max(-(-total // amount), total * loads[0] // sum(loads)))
    least = 1 if total - largest >= amount - 1 else 0
    holding, surplus = [largest] + [least] * (amount - 1), total - largest - least * (amount - 1)
    while surplus > 0:
        candidates = [i for i in range(1, amount) if holding[i] < largest] or [i for i in range(1, amount) if holding[i] < most]
        whole, remaining = sum([loads[i] for i in candidates]), surplus
        for i in candidates:
            extra = min(most - holding[i], max(1, remaining * loads[i] // whole), surplus)
            holding[i] = holding[i] + extra
            surplus = surplus - extra
    return np.array(holding)


def gaussian(rng, extent, scale, reach, shards=(), kind=jnp.bfloat16):
    level = block_scale(rng, extent, shards, -0.22, 0.18) if shards else 1.0
    values = jax.random.normal(rng, extent, jnp.float32) * scale * level
    return jnp.minimum(jnp.maximum(values, -reach), reach).astype(kind)


def setup_inputs(seed: int = 0) -> dict:
    streams_of = jax.random.split(jax.random.key(seed), 10)
    tokens = gaussian(streams_of[0], (TOKENS, D), 1.0, 6.0, ((0, 32),))
    routes_keys = jax.random.split(jax.random.fold_in(streams_of[1], 1), TOKENS // TOK_DEV)
    routes_turns = jax.random.permutation(jax.random.fold_in(streams_of[1], 3), TOKENS // TOK_DEV)
    routes = jax.vmap(lambda own, number: assign_block(jax.random.fold_in(streams_of[1], 2), own, number, TOK_DEV, EXPERTS, TOP, CAP, 2))(routes_keys, routes_turns).reshape((TOKENS, TOP))
    gates = jnp.clip(jnp.exp(math.log(0.5) - 2.3025851 * jax.random.uniform(streams_of[2], (TOKENS, TOP), jnp.float32) ** block_scale(streams_of[2], (TOKENS, TOP), ((0, 32),), -0.2, 0.2)), 0.05, 0.5)
    expert_gate = gaussian(streams_of[3], (EXPERTS, D, FF), D ** -0.5, 0.125, ((0, 32), (2, 8)))
    expert_up = gaussian(streams_of[4], (EXPERTS, D, FF), D ** -0.5, 0.125, ((0, 32), (2, 8)))
    expert_down = gaussian(streams_of[5], (EXPERTS, FF, D), FF ** -0.5, 0.15625, ((0, 32), (1, 8)))
    shared_gate = gaussian(streams_of[6], (D, SHARED_FF), D ** -0.5, 0.125, ((1, 8),))
    shared_up = gaussian(streams_of[7], (D, SHARED_FF), D ** -0.5, 0.125, ((1, 8),))
    shared_down = gaussian(streams_of[8], (SHARED_FF, D), SHARED_FF ** -0.5, 0.109375, ((0, 8),))
    return dict(tokens=tokens, routes=routes, gates=gates, expert_gate=expert_gate, expert_up=expert_up, expert_down=expert_down, shared_gate=shared_gate, shared_up=shared_up, shared_down=shared_down)


def slot_tables(routes, gates, experts, capacity):
    rows, top = routes.shape
    flat = routes.reshape(-1)
    onehot = (flat[:, None] == jnp.arange(experts, dtype=jnp.int32)[None, :]).astype(jnp.int32)
    before = jnp.cumsum(onehot, axis=0) - onehot
    rank = jnp.sum(before * onehot, axis=1).astype(jnp.int32)
    token_of = (jnp.arange(rows * top, dtype=jnp.int32) // top).astype(jnp.int32)
    slot_tok = jnp.zeros((experts, capacity), jnp.int32).at[flat, rank].set(token_of)
    slot_gate = jnp.zeros((experts, capacity), jnp.float32).at[flat, rank].set(gates.reshape(-1))
    return slot_tok, slot_gate


def reference(tokens, routes, gates, expert_gate, expert_up, expert_down, shared_gate, shared_up, shared_down):
    blocks = TOKENS // TOK_DEV
    slot_tok, slot_gate = jax.vmap(lambda r, g: slot_tables(r, g, EXPERTS, CAP))(
        routes.reshape(blocks, TOK_DEV, TOP), gates.reshape(blocks, TOK_DEV, TOP))
    offsets = (jnp.arange(blocks, dtype=jnp.int32) * TOK_DEV).astype(jnp.int32)[:, None, None]
    slot_tok = slot_tok + offsets
    share = FF // N_SEQ

    def one_expert(total, index):
        rows = slot_tok[:, index, :].reshape(-1)
        weights = slot_gate[:, index, :].reshape(-1)
        chosen = tokens[rows]
        gate = jnp.dot(chosen, expert_gate[index], preferred_element_type=jnp.float32)
        up = jnp.dot(chosen, expert_up[index], preferred_element_type=jnp.float32)
        hidden = (jax.nn.silu(gate) * up).astype(jnp.bfloat16)
        parts = jnp.einsum("rsf,sfd->srd", hidden.astype(jnp.float32).reshape(-1, N_SEQ, share),
                           expert_down[index].astype(jnp.float32).reshape(N_SEQ, share, D))
        rounded = lax.optimization_barrier(parts.astype(jnp.bfloat16))
        result = jnp.sum(rounded.astype(jnp.float32), axis=0)
        return total.at[rows].add(weights[:, None] * result), None

    total = jnp.zeros((TOKENS, D), jnp.float32)
    total, unused = lax.scan(one_expert, total, jnp.arange(EXPERTS, dtype=jnp.int32))
    sgate = jnp.dot(tokens, shared_gate, preferred_element_type=jnp.float32)
    sup = jnp.dot(tokens, shared_up, preferred_element_type=jnp.float32)
    shidden = (jax.nn.silu(sgate) * sup).astype(jnp.bfloat16)
    shared = jnp.dot(shidden, shared_down, preferred_element_type=jnp.float32)
    return (total + shared).astype(jnp.bfloat16)
```

```python
import functools
import jax
import jax.numpy as jnp
from jax import lax
from jax.experimental import pallas as pl
from jax.experimental.pallas import tpu as pltpu
from jax.sharding import PartitionSpec as P

MESH = pl.DeviceIdType.MESH
F32 = jnp.float32
BF16 = jnp.bfloat16
CAP = 32
NX = 4
NY = 4


def kernel(nz, ny, top, tokens, routes, gates, wg_h, wu_h, wd_h, sg_h, su_h, sd_h, out,
           wg, wu, wd, sg, su, sd, rank_m, gate_m, xout, arr, part, precv, total, thru, final,
           back, ret, acc,
           w_sem, l_sem, a_send, a_recv, x_send, xl_recv, xr_recv, h_send, hl_recv, hr_recv,
           c_send, c_recv, p_send, p_recv, f_send, fl_recv, fr_recv, g_send, gl_recv, gr_recv,
           r_send, r_recv):
    rows = tokens.shape[0]
    width = xout.shape[2]
    half = ny * CAP
    experts = xout.shape[0]
    block = 2 * half
    seq, exp = lax.axis_index("seq"), lax.axis_index("expert")
    x, c = seq // 2, seq % 2
    z, y = exp // ny, exp % ny
    right, left, across = (x + 1) % NX, (x + NX - 1) % NX, (x + 2) % NX
    to_right = (right * 2 + c, exp)
    to_left = (left * 2 + c, exp)
    to_core = (x * 2 + 1 - c, exp)

    def offset(k):
        step = (k + 1) // 2
        odd = k % 2
        return odd * step + (1 - odd) * ((nz - step) % nz)

    def remote(src, dst, send, recv, target):
        return pltpu.make_async_remote_copy(
            src_ref=src, dst_ref=dst, send_sem=send, recv_sem=recv,
            device_id=target, device_id_type=MESH)

    barrier = pltpu.get_barrier_semaphore()

    @pl.loop(1, nz * ny)
    def _(d):
        pl.semaphore_signal(barrier, inc=1, device_id=(seq, (exp + d) % (nz * ny)),
                            device_id_type=MESH)

    for target in (to_right, to_left, to_core):
        pl.semaphore_signal(barrier, inc=1, device_id=target, device_id_type=MESH)

    loads = [pltpu.make_async_copy(a, b, w_sem.at[i]) for i, (a, b) in enumerate(
        ((sg_h, sg), (su_h, su), (sd_h, sd), (wg_h, wg), (wu_h, wu), (wd_h, wd)))]
    for copy in loads:
        copy.start()

    eid = lax.broadcasted_iota(jnp.int32, (rows, experts), 1)
    chosen = jnp.zeros((rows, experts), F32)
    weight = jnp.zeros((rows, experts), F32)
    for k in range(top):
        hit = routes[:, k:k + 1] == eid
        chosen = chosen + jnp.where(hit, 1.0, 0.0)
        weight = weight + jnp.where(hit, gates[:, k:k + 1], 0.0)
    gate_m[...] = weight
    below = lax.broadcasted_iota(jnp.int32, (rows, rows), 0) > lax.broadcasted_iota(
        jnp.int32, (rows, rows), 1)
    rank = jnp.dot(jnp.where(below, 1.0, 0.0).astype(BF16), chosen.astype(BF16),
                   preferred_element_type=F32)
    rank_m[...] = jnp.where(chosen > 0.5, rank, -1.0).astype(BF16)

    pl.semaphore_wait(barrier, nz * ny - 1 + 3)

    def send_slots(k):
        zb = (z + offset(k)) % nz
        first = zb * (2 * ny)
        row = lax.broadcasted_iota(jnp.int32, (block, experts), 0)
        col = lax.broadcasted_iota(jnp.int32, (block, experts), 1)
        spread = jnp.where(row // CAP + first == col, 1.0, 0.0).astype(BF16)
        ranks = lax.dot_general(spread, rank_m[...], (((1,), (1,)), ((), ())),
                                preferred_element_type=F32)
        place = (lax.broadcasted_iota(jnp.int32, (block, rows), 0) % CAP).astype(F32)
        pick = jnp.where(ranks == place, 1.0, 0.0).astype(BF16)
        mine = tokens[:, pl.ds(pl.multiple_of(seq * width, width), width)]
        slots = jnp.dot(pick, mine, preferred_element_type=F32).astype(BF16)
        xout[pl.ds(first, 2 * ny)] = slots.reshape(2 * ny, CAP, width)
        for dy in range(ny):
            there = zb * ny + (y + dy) % ny
            src = xout.at[pl.ds(2 * there, 2)]
            dst = arr.at[x, c, k, :, dy * CAP:(dy + 1) * CAP, :]
            copy = remote(src, dst, a_send.at[k], a_recv.at[k], (seq, there))
            if dy:
                copy.start()
            else:
                @pl.when(k > 0)
                def _():
                    copy.start()

                @pl.when(k == 0)
                def _():
                    pltpu.make_async_copy(src, dst, l_sem.at[0]).start()

    def gather_neighbours(k):
        @pl.when(k == 0)
        def _():
            pltpu.make_async_copy(xout.at[0:2], arr.at[x, c, 0, :, 0:CAP, :], l_sem.at[0]).wait()
            rest = arr.at[x, c, 0, :, CAP:half, :]
            remote(rest, rest, a_send.at[0], a_recv.at[0], to_right).wait_recv()

        own = arr.at[x, c, k]

        @pl.when(k > 0)
        def _():
            remote(own, own, a_send.at[k], a_recv.at[k], to_right).wait_recv()

        remote(own, own, x_send.at[k], xl_recv.at[k], to_right).start()
        remote(own, own, x_send.at[k], xr_recv.at[k], to_left).start()
        remote(own, own, c_send.at[k], c_recv.at[k], to_core).start()

    def gather_across(k):
        from_left, from_right = arr.at[left, c, k], arr.at[right, c, k]
        remote(from_left, from_left, x_send.at[k], xl_recv.at[k], to_right).wait_recv()
        remote(from_left.at[0], from_left.at[0], h_send.at[k], hl_recv.at[k], to_right).start()
        remote(from_left, from_left, c_send.at[k], c_recv.at[k], to_core).start()
        remote(from_right, from_right, x_send.at[k], xr_recv.at[k], to_left).wait_recv()
        remote(from_right.at[1], from_right.at[1], h_send.at[k], hr_recv.at[k], to_left).start()
        remote(from_right, from_right, c_send.at[k], c_recv.at[k], to_core).start()

    def gather_core(k):
        far = arr.at[across, c, k]
        remote(far.at[0], far.at[0], h_send.at[k], hl_recv.at[k], to_right).wait_recv()
        remote(far.at[1], far.at[1], h_send.at[k], hr_recv.at[k], to_left).wait_recv()
        remote(far, far, c_send.at[k], c_recv.at[k], to_core).start()

    def send_part(j):
        remote(part.at[j], precv.at[j], p_send.at[j], p_recv.at[j], to_core).start()

    def down(hidden, weights):
        for parity, dst in ((1 - c, part), (c, total)):
            for xx in range(NX):
                cols = pl.ds(pl.multiple_of((2 * xx + parity) * width, width), width)
                value = jnp.dot(hidden, weights(cols), preferred_element_type=F32).astype(BF16)
                yield dst, xx, value

    def shared_part():
        for copy in loads[:3]:
            copy.wait()
        gate = jnp.dot(tokens[...], sg[...], preferred_element_type=F32)
        up = jnp.dot(tokens[...], su[...], preferred_element_type=F32)
        hidden = (gate / (1.0 + jnp.exp(-gate)) * up).astype(BF16)
        for dst, xx, value in down(hidden, lambda cols: sd[:, cols]):
            dst[0, xx] = value.reshape(2, half, width)
        send_part(0)

    def routed_part(k):
        @pl.when(k == 0)
        def _():
            for copy in loads[3:]:
                copy.wait()

        other = arr.at[:, 1 - c, k]
        remote(other, other, c_send.at[k], c_recv.at[k], to_core).wait_recv()
        for e in range(2):
            gate = jnp.zeros((half, wg.shape[2]), F32)
            up = jnp.zeros((half, wg.shape[2]), F32)
            for s in range(2 * NX):
                a = arr[s // 2, s % 2, k, e]
                gate = gate + jnp.dot(a, wg[e, s * width:(s + 1) * width],
                                      preferred_element_type=F32)
                up = up + jnp.dot(a, wu[e, s * width:(s + 1) * width],
                                  preferred_element_type=F32)
            hidden = (gate / (1.0 + jnp.exp(-gate)) * up).astype(BF16)
            for dst, xx, value in down(hidden, lambda cols: wd[e, :, cols]):
                dst[k + 1, xx, e] = value
        send_part(k + 1)

    def reduce_core(j):
        remote(part.at[j], precv.at[j], p_send.at[j], p_recv.at[j], to_core).wait_recv()

        def add(xx):
            total[j, xx] = (total[j, xx].astype(F32) + precv[j, xx].astype(F32)).astype(BF16)

        add(across)
        remote(total.at[j, across, 0], thru.at[0, j], f_send.at[j], fl_recv.at[j], to_right).start()
        remote(total.at[j, across, 1], thru.at[1, j], f_send.at[j], fr_recv.at[j], to_left).start()
        add(right)
        remote(total.at[j, right, 1], final.at[0, j, 1], g_send.at[j], gl_recv.at[j], to_right).start()
        add(left)
        remote(total.at[j, left, 0], final.at[1, j, 0], g_send.at[j], gr_recv.at[j], to_left).start()
        add(x)

    def reduce_across(j):
        remote(thru.at[0, j], thru.at[0, j], f_send.at[j], fl_recv.at[j], to_right).wait_recv()
        total[j, right, 0] = (total[j, right, 0].astype(F32) + thru[0, j].astype(F32)).astype(BF16)
        remote(total.at[j, right, 0], final.at[0, j, 0], g_send.at[j], gl_recv.at[j], to_right).start()
        remote(thru.at[1, j], thru.at[1, j], f_send.at[j], fr_recv.at[j], to_left).wait_recv()
        total[j, left, 1] = (total[j, left, 1].astype(F32) + thru[1, j].astype(F32)).astype(BF16)
        remote(total.at[j, left, 1], final.at[1, j, 1], g_send.at[j], gr_recv.at[j], to_left).start()

    def reduce_neighbours(j):
        remote(final.at[0, j], final.at[0, j], g_send.at[j], gl_recv.at[j], to_right).wait_recv()
        remote(final.at[1, j], final.at[1, j], g_send.at[j], gr_recv.at[j], to_left).wait_recv()
        value = total[j, x].astype(F32) + final[0, j].astype(F32) + final[1, j].astype(F32)

        @pl.when(j == 0)
        def _():
            acc[...] = value.reshape(rows, width)

        @pl.when(j > 0)
        def _():
            k = j - 1
            back[k] = value.astype(BF16)
            zb = (z + nz - offset(k)) % nz
            for dy in range(ny):
                there = zb * ny + (y + ny - dy) % ny
                src = back.at[k, :, dy * CAP:(dy + 1) * CAP, :]
                dst = ret.at[pl.ds(2 * exp, 2)]
                copy = remote(src, dst, r_send.at[k], r_recv.at[k], (seq, there))
                if dy:
                    copy.start()
                else:
                    @pl.when(k > 0)
                    def _():
                        copy.start()

                    @pl.when(k == 0)
                    def _():
                        pltpu.make_async_copy(src, dst, l_sem.at[1]).start()

    def combine(k):
        zb = (z + offset(k)) % nz
        first = zb * (2 * ny)

        @pl.when(k == 0)
        def _():
            pltpu.make_async_copy(ret.at[0:2], ret.at[0:2], l_sem.at[1]).wait()
            rest = ret.at[0:2 * ny - 2]
            remote(rest, rest, r_send.at[0], r_recv.at[0], to_right).wait_recv()

        @pl.when(k > 0)
        def _():
            rest = ret.at[0:2 * ny]
            remote(rest, rest, r_send.at[k], r_recv.at[k], to_right).wait_recv()

        row = lax.broadcasted_iota(jnp.int32, (experts, block), 0)
        col = lax.broadcasted_iota(jnp.int32, (experts, block), 1)
        spread = jnp.where(col // CAP + first == row, 1.0, 0.0).astype(BF16)
        ranks = jnp.dot(rank_m[...], spread, preferred_element_type=F32)
        place = (lax.broadcasted_iota(jnp.int32, (rows, block), 1) % CAP).astype(F32)
        here = ranks == place
        values = ret[pl.ds(first, 2 * ny)].reshape(block, width)
        left_over = gate_m[...]
        total_here = acc[...]
        for _ in range(2):
            piece = left_over.astype(BF16)
            left_over = left_over - piece.astype(F32)
            wide = jnp.dot(piece, spread, preferred_element_type=F32)
            mix = jnp.where(here, wide, 0.0).astype(BF16)
            total_here = total_here + jnp.dot(mix, values, preferred_element_type=F32)
        acc[...] = total_here

    def stage(body, index, count):
        @pl.when((index >= 0) & (index < count))
        def _():
            body(index)

    @pl.loop(0, nz + 7)
    def _(i):
        stage(send_slots, i, nz)
        stage(gather_neighbours, i - 1, nz)
        stage(gather_across, i - 2, nz)
        stage(gather_core, i - 3, nz)
        stage(reduce_neighbours, i - 5, nz + 1)
        stage(reduce_across, i - 4, nz + 1)
        stage(reduce_core, i - 3, nz + 1)

        @pl.when(i == 2)
        def _():
            shared_part()

        stage(routed_part, i - 3, nz)
        stage(combine, i - 7, nz)

    out[...] = acc[...].astype(out.dtype)

    @pl.loop(0, nz)
    def _(k):
        @pl.when(k == 0)
        def _():
            rest = xout.at[0:2 * ny - 2]
            remote(rest, rest, a_send.at[0], a_recv.at[0], to_right).wait_send()
            remote(rest, rest, r_send.at[0], r_recv.at[0], to_right).wait_send()

        @pl.when(k > 0)
        def _():
            rest = xout.at[0:2 * ny]
            remote(rest, rest, a_send.at[k], a_recv.at[k], to_right).wait_send()
            remote(rest, rest, r_send.at[k], r_recv.at[k], to_right).wait_send()

        two = arr.at[0:2, 0, k]
        remote(two, two, x_send.at[k], xl_recv.at[k], to_right).wait_send()
        one = arr.at[0, 0, k]
        remote(one, one, h_send.at[k], hl_recv.at[k], to_right).wait_send()
        four = arr.at[:, 0, k]
        remote(four, four, c_send.at[k], c_recv.at[k], to_core).wait_send()

    @pl.loop(0, nz + 1)
    def _(j):
        remote(part.at[j], precv.at[j], p_send.at[j], p_recv.at[j], to_core).wait_send()
        one = final.at[0, j]
        remote(one, one, f_send.at[j], fl_recv.at[j], to_right).wait_send()
        two = total.at[j, 0:2]
        remote(two, two, g_send.at[j], gl_recv.at[j], to_right).wait_send()


def layer(tokens, routes, gates, wg, wu, wd, sg, su, sd, nz):
    rows, width_all = tokens.shape
    width = width_all // (2 * NX)
    ny = lax.axis_size("expert") // nz
    experts = 2 * nz * ny
    half = ny * CAP
    assert rows == 2 * half
    dma = pltpu.SemaphoreType.DMA
    vm = pltpu.VMEM
    scratch = [vm(a.shape, BF16) for a in (wg, wu, wd, sg, su, sd)]
    scratch += [
        vm((rows, experts), BF16),
        vm((rows, experts), F32),
        vm((experts, CAP, width), BF16),
        vm((NX, 2, nz, 2, half, width), BF16),
        vm((nz + 1, NX, 2, half, width), BF16),
        vm((nz + 1, NX, 2, half, width), BF16),
        vm((nz + 1, NX, 2, half, width), BF16),
        vm((2, nz + 1, half, width), BF16),
        vm((2, nz + 1, 2, half, width), BF16),
        vm((nz, 2, half, width), BF16),
        vm((experts, CAP, width), BF16),
        vm((rows, width), F32),
    ]
    scratch += [dma((6,)), dma((2,))]
    scratch += [dma((nz,)) for _ in range(10)]
    scratch += [dma((nz + 1,)) for _ in range(8)]
    scratch += [dma((nz,)) for _ in range(2)]
    return pl.pallas_call(
        functools.partial(kernel, nz, ny, routes.shape[1]),
        out_shape=jax.ShapeDtypeStruct((rows, width), BF16),
        in_specs=[pl.BlockSpec(memory_space=pltpu.VMEM)] * 3
        + [pl.BlockSpec(memory_space=pl.ANY)] * 6,
        out_specs=pl.BlockSpec(memory_space=pltpu.VMEM),
        scratch_shapes=scratch,
        compiler_params=pltpu.CompilerParams(
            collective_id=0, has_side_effects=True, vmem_limit_bytes=60 * 1024 * 1024),
        cost_estimate=pl.CostEstimate(
            flops=7 * 10**9, bytes_accessed=12 * 10**6, transcendentals=10**6),
    )(tokens, routes, gates, wg, wu, wd, sg, su, sd)


def solution(mesh):
    nz = mesh.shape["expert"] // NY
    return jax.shard_map(
        functools.partial(layer, nz=nz),
        mesh=mesh,
        in_specs=(
            P("expert", None),
            P("expert", None),
            P("expert", None),
            P("expert", None, "seq"),
            P("expert", None, "seq"),
            P("expert", "seq", None),
            P(None, "seq"),
            P(None, "seq"),
            P("seq", None),
        ),
        out_specs=P("expert", "seq"),
        check_vma=False,
    )
```

```python
import functools
import jax
import jax.numpy as jnp
from jax import lax
from jax.experimental import pallas as pl
from jax.experimental.pallas import tpu as pltpu
from jax.sharding import PartitionSpec as P

MESH = pl.DeviceIdType.MESH
F32 = jnp.float32
BF16 = jnp.bfloat16
CAP = 32
NX = 4
NY = 4
PLAN = {8: ((4, -1, 0, 3, -3, 2, -2, 1), (0, 1), (0, -1))}
FLOW = (
    ("near", 1, 1, 1),
    ("sum1", 1, 1, 5),
    ("routed", 1, 1, 4),
    ("slots", 8, 1, 0),
    ("mix", 3, 2, 11),
    ("far", 1, 1, 2),
    ("core", 1, 1, 3),
    ("shared", 1, 1, 0),
    ("sum3", 1, 1, 6),
    ("sum2", 1, 1, 5),
)


def plan_of(nz):
    default = [0] + [d for k in range(1, nz) for d in (k, -k)][:nz - 1]
    plan = PLAN.get(nz, (tuple(default), (0, 1), (0, -1)))
    return [[d % nz for d in part] for part in plan]


def dot_nt(a, b):
    return lax.dot_general(a, b, (((1,), (1,)), ((), ())), preferred_element_type=F32)


def kernel(nz, ny, top, tokens, routes, gates, wg_h, wu_h, wd_h, sg_h, su_h, sd_h, out,
           wg, wu, wd, sg, su, sd, rank_t, rank_m, gate_m, xout, xwide, arr, part, precv, total, thru, final,
           back, ret, rwide, twide, acc,
           w_sem, l_sem, a_send, a_recv, x_send, xl_recv, xr_recv, h_send, hl_recv, hr_recv,
           c_send, c_recv, p_send, p_recv, f_send, fl_recv, fr_recv, g_send, gl_recv, gr_recv,
           r_send, r_recv):
    rows = tokens.shape[0]
    width = xout.shape[2]
    half = ny * CAP
    experts = xout.shape[0]
    block = 2 * half
    seq, exp = lax.axis_index("seq"), lax.axis_index("expert")
    x, c = seq // 2, seq % 2
    z, y = exp // ny, exp % ny
    right, left, across = (x + 1) % NX, (x + NX - 1) % NX, (x + 2) % NX
    to_right = (right * 2 + c, exp)
    to_left = (left * 2 + c, exp)
    to_core = (x * 2 + 1 - c, exp)

    order, *whole = plan_of(nz)
    zero = order.index(0)
    wide_out, wide_in = [sorted(order.index(d) for d in part) for part in whole]

    def offset(p):
        value = 0
        for q, d in enumerate(order):
            value = jnp.where(p == q, d, value)
        return value

    def within(p, some):
        hit = p == nz + 1
        for q in some:
            hit = hit | (p == q)
        return hit

    def remote(src, dst, send, recv, target):
        return pltpu.make_async_remote_copy(
            src_ref=src, dst_ref=dst, send_sem=send, recv_sem=recv,
            device_id=target, device_id_type=MESH)

    barrier = pltpu.get_barrier_semaphore()

    @pl.loop(1, nz * ny)
    def _(d):
        pl.semaphore_signal(barrier, inc=1, device_id=(seq, (exp + d) % (nz * ny)),
                            device_id_type=MESH)

    for target in (to_right, to_left, to_core):
        pl.semaphore_signal(barrier, inc=1, device_id=target, device_id_type=MESH)

    loads = [pltpu.make_async_copy(a, b, w_sem.at[i]) for i, (a, b) in enumerate(
        ((sg_h, sg), (su_h, su), (sd_h, sd), (wg_h, wg), (wu_h, wu), (wd_h, wd)))]
    for copy in loads:
        copy.start()

    eid = lax.broadcasted_iota(jnp.int32, (experts, rows), 0)
    chosen = jnp.zeros((experts, rows), F32)
    for k in range(top):
        chosen = chosen + jnp.where(routes[k:k + 1, :] == eid, 1.0, 0.0)
    row = lax.broadcasted_iota(jnp.int32, (rows, rows), 0)
    col = lax.broadcasted_iota(jnp.int32, (rows, rows), 1)
    before = jnp.where(row < col, 1.0, 0.0).astype(BF16)
    rank = jnp.dot(chosen.astype(BF16), before, preferred_element_type=F32)
    rank_t[...] = jnp.where(chosen > 0.5, rank, -1.0).astype(BF16)

    pl.semaphore_wait(barrier, nz * ny - 1 + 3)

    def send_one(src, dst, p, dy, send, recv, target, local):
        copy = remote(src, dst, send.at[p], recv.at[p], target)
        if dy:
            copy.start()
        else:
            @pl.when(p != zero)
            def _():
                copy.start()

            @pl.when(p == zero)
            def _():
                pltpu.make_async_copy(src, dst, l_sem.at[local]).start()

    def slots_stage(p):
        zb = (z + offset(p)) % nz
        first = zb * (2 * ny)
        row = lax.broadcasted_iota(jnp.int32, (block, experts), 0)
        col = lax.broadcasted_iota(jnp.int32, (block, experts), 1)
        spread = jnp.where(row // CAP + first == col, 1.0, 0.0).astype(BF16)
        ranks = jnp.dot(spread, rank_t[...], preferred_element_type=F32)
        place = (lax.broadcasted_iota(jnp.int32, (block, rows), 0) % CAP).astype(F32)
        pick = jnp.where(ranks == place, 1.0, 0.0).astype(BF16)

        def gathered(s):
            mine = tokens[:, pl.ds(pl.multiple_of(s * width, width), width)]
            slots = jnp.dot(pick, mine, preferred_element_type=F32).astype(BF16)
            return slots.reshape(2 * ny, CAP, width)

        @pl.when(jnp.logical_not(within(p, wide_out)))
        def _():
            xout[pl.ds(first, 2 * ny)] = gathered(seq)
            for dy in range(ny):
                there = zb * ny + (y + dy) % ny
                send_one(xout.at[pl.ds(2 * there, 2)],
                         arr.at[x, c, p, :, dy * CAP:(dy + 1) * CAP, :],
                         p, dy, a_send, a_recv, (seq, there), 0)

        for f, q in enumerate(wide_out):
            @pl.when(p == q)
            def _():
                for xx in range(NX):
                    xwide[f, xx] = gathered(2 * xx + c)
                for dy in range(ny):
                    yy = (y + dy) % ny
                    send_one(xwide.at[f, :, pl.ds(2 * yy, 2)],
                             arr.at[:, c, p, :, dy * CAP:(dy + 1) * CAP, :],
                             p, dy, a_send, a_recv, (seq, zb * ny + yy), 0)

    def arrived(p, all_of, rest_of, recv, local):
        @pl.when(p != zero)
        def _():
            remote(all_of, all_of, a_send.at[p], recv.at[p], to_right).wait_recv()

        @pl.when(p == zero)
        def _():
            first = all_of.at[(slice(None),) * (len(all_of.shape) - 3)
                              + ((slice(None), slice(0, CAP)) if local == 0 else (slice(0, 2),))]
            pltpu.make_async_copy(first, first, l_sem.at[local]).wait()
            remote(rest_of, rest_of, a_send.at[p], recv.at[p], to_right).wait_recv()

    def near_stage(p):
        @pl.when(within(p, wide_out))
        def _():
            own = arr.at[:, c, p]
            arrived(p, own, arr.at[:, c, p, :, CAP:half, :], a_recv, 0)
            remote(own, own, c_send.at[p], c_recv.at[p], to_core).start()

        @pl.when(jnp.logical_not(within(p, wide_out)))
        def _():
            own = arr.at[x, c, p]
            arrived(p, own, arr.at[x, c, p, :, CAP:half, :], a_recv, 0)
            remote(own, own, x_send.at[p], xl_recv.at[p], to_right).start()
            remote(own, own, x_send.at[p], xr_recv.at[p], to_left).start()
            remote(own, own, c_send.at[p], c_recv.at[p], to_core).start()

    def far_stage(p):
        @pl.when(jnp.logical_not(within(p, wide_out)))
        def _():
            from_left, from_right = arr.at[left, c, p], arr.at[right, c, p]
            remote(from_left, from_left, x_send.at[p], xl_recv.at[p], to_right).wait_recv()
            remote(from_left.at[0], from_left.at[0], h_send.at[p], hl_recv.at[p], to_right).start()
            remote(from_left, from_left, c_send.at[p], c_recv.at[p], to_core).start()
            remote(from_right, from_right, x_send.at[p], xr_recv.at[p], to_left).wait_recv()
            remote(from_right.at[1], from_right.at[1], h_send.at[p], hr_recv.at[p], to_left).start()
            remote(from_right, from_right, c_send.at[p], c_recv.at[p], to_core).start()

    def core_stage(p):
        @pl.when(jnp.logical_not(within(p, wide_out)))
        def _():
            far = arr.at[across, c, p]
            remote(far.at[0], far.at[0], h_send.at[p], hl_recv.at[p], to_right).wait_recv()
            remote(far.at[1], far.at[1], h_send.at[p], hr_recv.at[p], to_left).wait_recv()
            remote(far, far, c_send.at[p], c_recv.at[p], to_core).start()

    def send_part(j):
        remote(part.at[j], precv.at[j], p_send.at[j], p_recv.at[j], to_core).start()

    def down(hidden, weights):
        for parity, dst in ((1 - c, part), (c, total)):
            for xx in range(NX):
                cols = pl.ds(pl.multiple_of((2 * xx + parity) * width, width), width)
                value = jnp.dot(hidden, weights(cols), preferred_element_type=F32).astype(BF16)
                yield dst, xx, value

    def turn_tables():
        eid = lax.broadcasted_iota(jnp.int32, (experts, rows), 0)
        weight = jnp.zeros((experts, rows), F32)
        for k in range(top):
            weight = weight + jnp.where(routes[k:k + 1, :] == eid, gates[k:k + 1, :], 0.0)
        row = lax.broadcasted_iota(jnp.int32, (rows, rows), 0)
        col = lax.broadcasted_iota(jnp.int32, (rows, rows), 1)
        same = jnp.where(row == col, 1.0, 0.0).astype(BF16)
        high = weight.astype(BF16)
        low = (weight - high.astype(F32)).astype(BF16)
        rank_m[...] = dot_nt(same, rank_t[...]).astype(BF16)
        gate_m[0] = dot_nt(same, high).astype(BF16)
        gate_m[1] = dot_nt(same, low).astype(BF16)

    def shared_stage(_):
        turn_tables()
        for copy in loads[:3]:
            copy.wait()
        gate = dot_nt(tokens[...], sg[...])
        up = dot_nt(tokens[...], su[...])
        hidden = (gate / (1.0 + jnp.exp(-gate)) * up).astype(BF16)
        for dst, xx, value in down(hidden, lambda cols: sd[:, cols]):
            dst[nz, xx] = value.reshape(2, half, width)
        send_part(nz)

    def routed_stage(p):
        @pl.when(p == 0)
        def _():
            for copy in loads[3:]:
                copy.wait()

        other = arr.at[:, 1 - c, p]
        remote(other, other, c_send.at[p], c_recv.at[p], to_core).wait_recv()
        for e in range(2):
            gate = jnp.zeros((half, wg.shape[1]), F32)
            up = jnp.zeros((half, wg.shape[1]), F32)
            for s in range(2 * NX):
                a = arr[s // 2, s % 2, p, e]
                gate = gate + dot_nt(a, wg[e, :, s * width:(s + 1) * width])
                up = up + dot_nt(a, wu[e, :, s * width:(s + 1) * width])
            hidden = (gate / (1.0 + jnp.exp(-gate)) * up).astype(BF16)
            for dst, xx, value in down(hidden, lambda cols: wd[e, :, cols]):
                dst[p, xx, e] = value
        send_part(p)

    def sum1_stage(j):
        remote(part.at[j], precv.at[j], p_send.at[j], p_recv.at[j], to_core).wait_recv()

        def add(xx):
            value = total[j, xx].astype(F32) + precv[j, xx].astype(F32)
            if not wide_in:
                total[j, xx] = value.astype(BF16)
                return

            @pl.when(j < nz)
            def _():
                total[j, xx] = value.astype(BF16)

            @pl.when(j == nz)
            def _():
                total[j, xx] = (value + twide[xx].reshape(2, half, width)).astype(BF16)

        @pl.when(jnp.logical_not(within(j, wide_in)))
        def _():
            add(across)
            remote(total.at[j, across, 0], thru.at[0, j], f_send.at[j], fl_recv.at[j], to_right).start()
            remote(total.at[j, across, 1], thru.at[1, j], f_send.at[j], fr_recv.at[j], to_left).start()
            add(right)
            remote(total.at[j, right, 1], final.at[0, j, 1], g_send.at[j], gl_recv.at[j], to_right).start()
            add(left)
            remote(total.at[j, left, 0], final.at[1, j, 0], g_send.at[j], gr_recv.at[j], to_left).start()
            add(x)

        for f, q in enumerate(wide_in):
            @pl.when(j == q)
            def _():
                for xx in range(NX):
                    total[q, xx] = (total[q, xx].astype(F32) + precv[q, xx].astype(F32)).astype(BF16)
                zb = (z + nz - order[q]) % nz
                for dy in range(ny):
                    there = zb * ny + (y + ny - dy) % ny
                    send_one(total.at[q, :, :, dy * CAP:(dy + 1) * CAP, :],
                             rwide.at[f, :, pl.ds(2 * y, 2)],
                             j, dy, r_send, r_recv, (seq, there), 1)

    def sum2_stage(j):
        @pl.when(jnp.logical_not(within(j, wide_in)))
        def _():
            remote(thru.at[0, j], thru.at[0, j], f_send.at[j], fl_recv.at[j], to_right).wait_recv()
            total[j, right, 0] = (total[j, right, 0].astype(F32) + thru[0, j].astype(F32)).astype(BF16)
            remote(total.at[j, right, 0], final.at[0, j, 0], g_send.at[j], gl_recv.at[j], to_right).start()
            remote(thru.at[1, j], thru.at[1, j], f_send.at[j], fr_recv.at[j], to_left).wait_recv()
            total[j, left, 1] = (total[j, left, 1].astype(F32) + thru[1, j].astype(F32)).astype(BF16)
            remote(total.at[j, left, 1], final.at[1, j, 1], g_send.at[j], gr_recv.at[j], to_left).start()

    def sum3_stage(j):
        @pl.when(jnp.logical_not(within(j, wide_in)))
        def _():
            remote(final.at[0, j], final.at[0, j], g_send.at[j], gl_recv.at[j], to_right).wait_recv()
            remote(final.at[1, j], final.at[1, j], g_send.at[j], gr_recv.at[j], to_left).wait_recv()
            value = total[j, x].astype(F32) + final[0, j].astype(F32) + final[1, j].astype(F32)

            @pl.when(j == nz)
            def _():
                acc[...] = acc[...] + value.reshape(rows, width)

            @pl.when(j < nz)
            def _():
                back[j] = value.astype(BF16)
                zb = (z + nz - offset(j)) % nz
                for dy in range(ny):
                    there = zb * ny + (y + ny - dy) % ny
                    send_one(back.at[j, :, dy * CAP:(dy + 1) * CAP, :], ret.at[pl.ds(2 * exp, 2)],
                             j, dy, r_send, r_recv, (seq, there), 1)

    def mix_stage(p):
        zb = (z + offset(p)) % nz
        first = zb * (2 * ny)

        row = lax.broadcasted_iota(jnp.int32, (experts, block), 0)
        col = lax.broadcasted_iota(jnp.int32, (experts, block), 1)
        spread = jnp.where(col // CAP + first == row, 1.0, 0.0).astype(BF16)
        ranks = jnp.dot(rank_m[...], spread, preferred_element_type=F32)
        place = (lax.broadcasted_iota(jnp.int32, (rows, block), 1) % CAP).astype(F32)
        here = ranks == place
        pieces = [jnp.where(here, jnp.dot(gate_m[piece], spread, preferred_element_type=F32),
                            0.0).astype(BF16) for piece in range(2)]

        def mixed(values):
            values = values.reshape(block, width)
            return sum(jnp.dot(piece, values, preferred_element_type=F32) for piece in pieces)

        @pl.when(jnp.logical_not(within(p, wide_in)))
        def _():
            arrived(p, ret.at[0:2 * ny], ret.at[0:2 * ny - 2], r_recv, 1)
            acc[...] = acc[...] + mixed(ret[pl.ds(first, 2 * ny)])

        for f, q in enumerate(wide_in):
            @pl.when(p == q)
            def _():
                arrived(p, rwide.at[f], rwide.at[f, :, 0:2 * ny - 2], r_recv, 1)
                for xx in range(NX):
                    if f == 0:
                        twide[xx] = mixed(rwide[f, xx])
                    else:
                        twide[xx] = twide[xx] + mixed(rwide[f, xx])

    stages = {
        "slots": (slots_stage, nz), "near": (near_stage, nz), "far": (far_stage, nz),
        "core": (core_stage, nz), "shared": (shared_stage, 1), "routed": (routed_stage, nz),
        "sum1": (sum1_stage, nz + 1), "sum2": (sum2_stage, nz + 1), "sum3": (sum3_stage, nz + 1),
        "mix": (mix_stage, nz),
    }
    last = max(first + -(-stages[name][1] * den // num) for name, num, den, first in FLOW)
    acc[...] = jnp.zeros_like(acc)

    @pl.loop(0, last)
    def _(i):
        for name, num, den, first in FLOW:
            body, count = stages[name]

            def reached(steps):
                return jnp.minimum(num * jnp.maximum(steps, 0) // den, count)

            pl.loop(reached(i - first), reached(i + 1 - first))(body)

    out[...] = acc[...].astype(out.dtype)

    for p in range(nz):
        skip = 2 if p == zero else 0

        def sent(narrow, some, broad):
            if p in some:
                return broad.at[some.index(p), :, 0:2 * ny - skip]
            return narrow.at[0:2 * ny - skip]

        out_part, in_part = sent(xout, wide_out, xwide), sent(ret, wide_in, rwide)
        remote(out_part, out_part, a_send.at[p], a_recv.at[p], to_right).wait_send()
        remote(in_part, in_part, r_send.at[p], r_recv.at[p], to_right).wait_send()
        four = arr.at[:, 0, p]
        remote(four, four, c_send.at[p], c_recv.at[p], to_core).wait_send()
        if p not in wide_out:
            two, one = arr.at[0:2, 0, p], arr.at[0, 0, p]
            remote(two, two, x_send.at[p], xl_recv.at[p], to_right).wait_send()
            remote(one, one, h_send.at[p], hl_recv.at[p], to_right).wait_send()
    for j in range(nz + 1):
        remote(part.at[j], precv.at[j], p_send.at[j], p_recv.at[j], to_core).wait_send()
        if j not in wide_in:
            one, two = final.at[0, j], total.at[j, 0:2]
            remote(one, one, f_send.at[j], fl_recv.at[j], to_right).wait_send()
            remote(two, two, g_send.at[j], gl_recv.at[j], to_right).wait_send()


def layer(tokens, routes, gates, wg, wu, wd, sg, su, sd, nz):
    rows, width_all = tokens.shape
    routes, gates, sg, su = routes.T, gates.T, sg.T, su.T
    wg, wu = wg.transpose(0, 2, 1), wu.transpose(0, 2, 1)
    width = width_all // (2 * NX)
    ny = lax.axis_size("expert") // nz
    experts = 2 * nz * ny
    half = ny * CAP
    out_wide, in_wide = [max(len(part), 1) for part in plan_of(nz)[1:]]
    assert rows == 2 * half
    dma = pltpu.SemaphoreType.DMA
    vm = pltpu.VMEM
    scratch = [vm(a.shape, BF16) for a in (wg, wu, wd, sg, su, sd)]
    scratch += [
        vm((experts, rows), BF16),
        vm((rows, experts), BF16),
        vm((2, rows, experts), BF16),
        vm((experts, CAP, width), BF16),
        vm((out_wide, NX, 2 * ny, CAP, width), BF16),
        vm((NX, 2, nz, 2, half, width), BF16),
        vm((nz + 1, NX, 2, half, width), BF16),
        vm((nz + 1, NX, 2, half, width), BF16),
        vm((nz + 1, NX, 2, half, width), BF16),
        vm((2, nz + 1, half, width), BF16),
        vm((2, nz + 1, 2, half, width), BF16),
        vm((nz, 2, half, width), BF16),
        vm((experts, CAP, width), BF16),
        vm((in_wide, NX, 2 * ny, CAP, width), BF16),
        vm((NX, rows, width), F32),
        vm((rows, width), F32),
    ]
    scratch += [dma((6,)), dma((2,))]
    scratch += [dma((nz,)) for _ in range(10)]
    scratch += [dma((nz + 1,)) for _ in range(8)]
    scratch += [dma((nz,)) for _ in range(2)]
    return pl.pallas_call(
        functools.partial(kernel, nz, ny, routes.shape[0]),
        out_shape=jax.ShapeDtypeStruct((rows, width), BF16),
        in_specs=[pl.BlockSpec(memory_space=pltpu.VMEM)] * 3
        + [pl.BlockSpec(memory_space=pl.ANY)] * 6,
        out_specs=pl.BlockSpec(memory_space=pltpu.VMEM),
        scratch_shapes=scratch,
        compiler_params=pltpu.CompilerParams(
            collective_id=0, has_side_effects=True, vmem_limit_bytes=60 * 1024 * 1024),
        cost_estimate=pl.CostEstimate(
            flops=7 * 10**9, bytes_accessed=12 * 10**6, transcendentals=10**6),
    )(tokens, routes, gates, wg, wu, wd, sg, su, sd)


def solution(mesh):
    nz = mesh.shape["expert"] // NY
    return jax.shard_map(
        functools.partial(layer, nz=nz),
        mesh=mesh,
        in_specs=(
            P("expert", None),
            P("expert", None),
            P("expert", None),
            P("expert", None, "seq"),
            P("expert", None, "seq"),
            P("expert", "seq", None),
            P(None, "seq"),
            P(None, "seq"),
            P("seq", None),
        ),
        out_specs=P("expert", "seq"),
        check_vma=False,
    )
```

```python
import functools
import jax
import jax.numpy as jnp
from jax import lax
from jax.experimental import pallas as pl
from jax.experimental.pallas import tpu as pltpu
from jax.sharding import PartitionSpec as P

MESH = pl.DeviceIdType.MESH
F32 = jnp.float32
BF16 = jnp.bfloat16
CAP = 32
NX = 4
NY = 4
EARLY = 8
PLAN = {8: ((4, -1, 0, 3, -3, 2, -2, 1), (0, 1), (0, -1))}
FLOW = (
    ("near", 1, 1, 1),
    ("sum1", 1, 1, 5),
    ("routed", 1, 1, 4),
    ("slots", 8, 1, 0),
    ("mix", 3, 2, 11),
    ("far", 1, 1, 2),
    ("core", 1, 1, 3),
    ("shared", 1, 1, 0),
    ("sum3", 1, 1, 6),
    ("sum2", 1, 1, 5),
)


def plan_of(nz):
    default = [0] + [d for k in range(1, nz) for d in (k, -k)][:nz - 1]
    plan = PLAN.get(nz, (tuple(default), (0, 1), (0, -1)))
    return [[d % nz for d in part] for part in plan]


def dot_nt(a, b):
    return lax.dot_general(a, b, (((1,), (1,)), ((), ())), preferred_element_type=F32)


def kernel(nz, ny, top, tokens_h, routes_h, gates_h, wg_h, wu_h, wd_h, sg_h, su_h, sd_h, out,
           tokens, routes, gates, wg, wu, wd, sg, su, sd, rank_t, rank_m, gate_m, xout, xwide, arr, part, precv, total, thru, final,
           back, ret, rwide, twide, acc,
           w_sem, l_sem, a_send, a_recv, x_send, xl_recv, xr_recv, h_send, hl_recv, hr_recv,
           c_send, c_recv, p_send, p_recv, f_send, fl_recv, fr_recv, g_send, gl_recv, gr_recv,
           r_send, r_recv):
    rows = tokens.shape[0]
    width = xout.shape[2]
    half = ny * CAP
    experts = xout.shape[0]
    block = 2 * half
    seq, exp = lax.axis_index("seq"), lax.axis_index("expert")
    x, c = seq // 2, seq % 2
    z, y = exp // ny, exp % ny
    right, left, across = (x + 1) % NX, (x + NX - 1) % NX, (x + 2) % NX
    to_right = (right * 2 + c, exp)
    to_left = (left * 2 + c, exp)
    to_core = (x * 2 + 1 - c, exp)

    order, *whole = plan_of(nz)
    zero = order.index(0)
    wide_out, wide_in = [sorted(order.index(d) for d in part) for part in whole]

    def offset(p):
        value = 0
        for q, d in enumerate(order):
            value = jnp.where(p == q, d, value)
        return value

    def within(p, some):
        hit = p == nz + 1
        for q in some:
            hit = hit | (p == q)
        return hit

    def remote(src, dst, send, recv, target):
        return pltpu.make_async_remote_copy(
            src_ref=src, dst_ref=dst, send_sem=send, recv_sem=recv,
            device_id=target, device_id_type=MESH)

    small = [pltpu.make_async_copy(a, b, w_sem.at[6 + i]) for i, (a, b) in enumerate(
        ((routes_h, routes), (tokens_h, tokens), (gates_h, gates)))]
    for copy in small:
        copy.start()

    barrier = pltpu.get_barrier_semaphore()

    @pl.loop(1, nz * ny)
    def _(d):
        pl.semaphore_signal(barrier, inc=1, device_id=(seq, (exp + d) % (nz * ny)),
                            device_id_type=MESH)

    for target in (to_right, to_left, to_core):
        pl.semaphore_signal(barrier, inc=1, device_id=target, device_id_type=MESH)

    loads = [pltpu.make_async_copy(a, b, w_sem.at[i]) for i, (a, b) in enumerate(
        ((sg_h, sg), (su_h, su), (sd_h, sd), (wg_h, wg), (wu_h, wu), (wd_h, wd)))]
    small[0].wait()

    eid = lax.broadcasted_iota(jnp.int32, (experts, rows), 0)
    chosen = jnp.zeros((experts, rows), F32)
    for k in range(top):
        chosen = chosen + jnp.where(routes[k:k + 1, :] == eid, 1.0, 0.0)
    row = lax.broadcasted_iota(jnp.int32, (rows, rows), 0)
    col = lax.broadcasted_iota(jnp.int32, (rows, rows), 1)
    before = jnp.where(row < col, 1.0, 0.0).astype(BF16)
    rank = jnp.dot(chosen.astype(BF16), before, preferred_element_type=F32)
    rank_t[...] = jnp.where(chosen > 0.5, rank, -1.0).astype(BF16)

    def send_one(src, dst, p, dy, send, recv, target, local):
        copy = remote(src, dst, send.at[p], recv.at[p], target)
        if dy:
            copy.start()
        else:
            @pl.when(p != zero)
            def _():
                copy.start()

            @pl.when(p == zero)
            def _():
                pltpu.make_async_copy(src, dst, l_sem.at[local]).start()

    def fill_slots(p):
        zb = (z + offset(p)) % nz
        first = zb * (2 * ny)
        row = lax.broadcasted_iota(jnp.int32, (block, experts), 0)
        col = lax.broadcasted_iota(jnp.int32, (block, experts), 1)
        spread = jnp.where(row // CAP + first == col, 1.0, 0.0).astype(BF16)
        ranks = jnp.dot(spread, rank_t[...], preferred_element_type=F32)
        place = (lax.broadcasted_iota(jnp.int32, (block, rows), 0) % CAP).astype(F32)
        pick = jnp.where(ranks == place, 1.0, 0.0).astype(BF16)

        def gathered(s):
            mine = tokens[:, pl.ds(pl.multiple_of(s * width, width), width)]
            slots = jnp.dot(pick, mine, preferred_element_type=F32).astype(BF16)
            return slots.reshape(2 * ny, CAP, width)

        @pl.when(jnp.logical_not(within(p, wide_out)))
        def _():
            xout[pl.ds(first, 2 * ny)] = gathered(seq)

        for f, q in enumerate(wide_out):
            @pl.when(p == q)
            def _():
                for xx in range(NX):
                    xwide[f, xx] = gathered(2 * xx + c)

    def slots_stage(p):
        zb = (z + offset(p)) % nz

        @pl.when(p >= EARLY)
        def _():
            fill_slots(p)

        @pl.when(jnp.logical_not(within(p, wide_out)))
        def _():
            for dy in range(ny):
                there = zb * ny + (y + dy) % ny
                send_one(xout.at[pl.ds(2 * there, 2)],
                         arr.at[x, c, p, :, dy * CAP:(dy + 1) * CAP, :],
                         p, dy, a_send, a_recv, (seq, there), 0)

        for f, q in enumerate(wide_out):
            @pl.when(p == q)
            def _():
                for dy in range(ny):
                    yy = (y + dy) % ny
                    send_one(xwide.at[f, :, pl.ds(2 * yy, 2)],
                             arr.at[:, c, p, :, dy * CAP:(dy + 1) * CAP, :],
                             p, dy, a_send, a_recv, (seq, zb * ny + yy), 0)

    small[1].wait()
    for copy in loads:
        copy.start()
    pl.loop(0, min(EARLY, nz))(fill_slots)
    pl.semaphore_wait(barrier, nz * ny - 1 + 3)

    def arrived(p, all_of, rest_of, recv, local):
        @pl.when(p != zero)
        def _():
            remote(all_of, all_of, a_send.at[p], recv.at[p], to_right).wait_recv()

        @pl.when(p == zero)
        def _():
            first = all_of.at[(slice(None),) * (len(all_of.shape) - 3)
                              + ((slice(None), slice(0, CAP)) if local == 0 else (slice(0, 2),))]
            pltpu.make_async_copy(first, first, l_sem.at[local]).wait()
            remote(rest_of, rest_of, a_send.at[p], recv.at[p], to_right).wait_recv()

    def near_stage(p):
        @pl.when(within(p, wide_out))
        def _():
            own = arr.at[:, c, p]
            arrived(p, own, arr.at[:, c, p, :, CAP:half, :], a_recv, 0)
            remote(own, own, c_send.at[p], c_recv.at[p], to_core).start()

        @pl.when(jnp.logical_not(within(p, wide_out)))
        def _():
            own = arr.at[x, c, p]
            arrived(p, own, arr.at[x, c, p, :, CAP:half, :], a_recv, 0)
            remote(own, own, x_send.at[p], xl_recv.at[p], to_right).start()
            remote(own, own, x_send.at[p], xr_recv.at[p], to_left).start()
            remote(own, own, c_send.at[p], c_recv.at[p], to_core).start()

    def far_stage(p):
        @pl.when(jnp.logical_not(within(p, wide_out)))
        def _():
            from_left, from_right = arr.at[left, c, p], arr.at[right, c, p]
            remote(from_left, from_left, x_send.at[p], xl_recv.at[p], to_right).wait_recv()
            remote(from_left.at[0], from_left.at[0], h_send.at[p], hl_recv.at[p], to_right).start()
            remote(from_left, from_left, c_send.at[p], c_recv.at[p], to_core).start()
            remote(from_right, from_right, x_send.at[p], xr_recv.at[p], to_left).wait_recv()
            remote(from_right.at[1], from_right.at[1], h_send.at[p], hr_recv.at[p], to_left).start()
            remote(from_right, from_right, c_send.at[p], c_recv.at[p], to_core).start()

    def core_stage(p):
        @pl.when(jnp.logical_not(within(p, wide_out)))
        def _():
            far = arr.at[across, c, p]
            remote(far.at[0], far.at[0], h_send.at[p], hl_recv.at[p], to_right).wait_recv()
            remote(far.at[1], far.at[1], h_send.at[p], hr_recv.at[p], to_left).wait_recv()
            remote(far, far, c_send.at[p], c_recv.at[p], to_core).start()

    def send_part(j):
        remote(part.at[j], precv.at[j], p_send.at[j], p_recv.at[j], to_core).start()

    def down(hidden, weights):
        for parity, dst in ((1 - c, part), (c, total)):
            for xx in range(NX):
                cols = pl.ds(pl.multiple_of((2 * xx + parity) * width, width), width)
                value = jnp.dot(hidden, weights(cols), preferred_element_type=F32).astype(BF16)
                yield dst, xx, value

    def turn_tables():
        small[2].wait()
        eid = lax.broadcasted_iota(jnp.int32, (experts, rows), 0)
        weight = jnp.zeros((experts, rows), F32)
        for k in range(top):
            weight = weight + jnp.where(routes[k:k + 1, :] == eid, gates[k:k + 1, :], 0.0)
        row = lax.broadcasted_iota(jnp.int32, (rows, rows), 0)
        col = lax.broadcasted_iota(jnp.int32, (rows, rows), 1)
        same = jnp.where(row == col, 1.0, 0.0).astype(BF16)
        high = weight.astype(BF16)
        low = (weight - high.astype(F32)).astype(BF16)
        rank_m[...] = dot_nt(same, rank_t[...]).astype(BF16)
        gate_m[0] = dot_nt(same, high).astype(BF16)
        gate_m[1] = dot_nt(same, low).astype(BF16)

    def shared_stage(_):
        turn_tables()
        for copy in loads[:3]:
            copy.wait()
        gate = dot_nt(tokens[...], sg[...])
        up = dot_nt(tokens[...], su[...])
        hidden = (gate / (1.0 + jnp.exp(-gate)) * up).astype(BF16)
        for dst, xx, value in down(hidden, lambda cols: sd[:, cols]):
            dst[nz, xx] = value.reshape(2, half, width)
        send_part(nz)

    def routed_stage(p):
        @pl.when(p == 0)
        def _():
            for copy in loads[3:]:
                copy.wait()

        other = arr.at[:, 1 - c, p]
        remote(other, other, c_send.at[p], c_recv.at[p], to_core).wait_recv()
        for e in range(2):
            gate = jnp.zeros((half, wg.shape[1]), F32)
            up = jnp.zeros((half, wg.shape[1]), F32)
            for s in range(2 * NX):
                a = arr[s // 2, s % 2, p, e]
                gate = gate + dot_nt(a, wg[e, :, s * width:(s + 1) * width])
                up = up + dot_nt(a, wu[e, :, s * width:(s + 1) * width])
            hidden = (gate / (1.0 + jnp.exp(-gate)) * up).astype(BF16)
            for dst, xx, value in down(hidden, lambda cols: wd[e, :, cols]):
                dst[p, xx, e] = value
        send_part(p)

    def sum1_stage(j):
        remote(part.at[j], precv.at[j], p_send.at[j], p_recv.at[j], to_core).wait_recv()

        def add(xx):
            value = total[j, xx].astype(F32) + precv[j, xx].astype(F32)
            if not wide_in:
                total[j, xx] = value.astype(BF16)
                return

            @pl.when(j < nz)
            def _():
                total[j, xx] = value.astype(BF16)

            @pl.when(j == nz)
            def _():
                total[j, xx] = (value + twide[xx].reshape(2, half, width)).astype(BF16)

        @pl.when(jnp.logical_not(within(j, wide_in)))
        def _():
            add(across)
            remote(total.at[j, across, 0], thru.at[0, j], f_send.at[j], fl_recv.at[j], to_right).start()
            remote(total.at[j, across, 1], thru.at[1, j], f_send.at[j], fr_recv.at[j], to_left).start()
            add(right)
            remote(total.at[j, right, 1], final.at[0, j, 1], g_send.at[j], gl_recv.at[j], to_right).start()
            add(left)
            remote(total.at[j, left, 0], final.at[1, j, 0], g_send.at[j], gr_recv.at[j], to_left).start()
            add(x)

        for f, q in enumerate(wide_in):
            @pl.when(j == q)
            def _():
                for xx in range(NX):
                    total[q, xx] = (total[q, xx].astype(F32) + precv[q, xx].astype(F32)).astype(BF16)
                zb = (z + nz - order[q]) % nz
                for dy in range(ny):
                    there = zb * ny + (y + ny - dy) % ny
                    send_one(total.at[q, :, :, dy * CAP:(dy + 1) * CAP, :],
                             rwide.at[f, :, pl.ds(2 * y, 2)],
                             j, dy, r_send, r_recv, (seq, there), 1)

    def sum2_stage(j):
        @pl.when(jnp.logical_not(within(j, wide_in)))
        def _():
            remote(thru.at[0, j], thru.at[0, j], f_send.at[j], fl_recv.at[j], to_right).wait_recv()
            total[j, right, 0] = (total[j, right, 0].astype(F32) + thru[0, j].astype(F32)).astype(BF16)
            remote(total.at[j, right, 0], final.at[0, j, 0], g_send.at[j], gl_recv.at[j], to_right).start()
            remote(thru.at[1, j], thru.at[1, j], f_send.at[j], fr_recv.at[j], to_left).wait_recv()
            total[j, left, 1] = (total[j, left, 1].astype(F32) + thru[1, j].astype(F32)).astype(BF16)
            remote(total.at[j, left, 1], final.at[1, j, 1], g_send.at[j], gr_recv.at[j], to_left).start()

    def sum3_stage(j):
        @pl.when(jnp.logical_not(within(j, wide_in)))
        def _():
            remote(final.at[0, j], final.at[0, j], g_send.at[j], gl_recv.at[j], to_right).wait_recv()
            remote(final.at[1, j], final.at[1, j], g_send.at[j], gr_recv.at[j], to_left).wait_recv()
            value = total[j, x].astype(F32) + final[0, j].astype(F32) + final[1, j].astype(F32)

            @pl.when(j == nz)
            def _():
                acc[...] = acc[...] + value.reshape(rows, width)

            @pl.when(j < nz)
            def _():
                back[j] = value.astype(BF16)
                zb = (z + nz - offset(j)) % nz
                for dy in range(ny):
                    there = zb * ny + (y + ny - dy) % ny
                    send_one(back.at[j, :, dy * CAP:(dy + 1) * CAP, :], ret.at[pl.ds(2 * exp, 2)],
                             j, dy, r_send, r_recv, (seq, there), 1)

    def mix_stage(p):
        zb = (z + offset(p)) % nz
        first = zb * (2 * ny)

        row = lax.broadcasted_iota(jnp.int32, (experts, block), 0)
        col = lax.broadcasted_iota(jnp.int32, (experts, block), 1)
        spread = jnp.where(col // CAP + first == row, 1.0, 0.0).astype(BF16)
        ranks = jnp.dot(rank_m[...], spread, preferred_element_type=F32)
        place = (lax.broadcasted_iota(jnp.int32, (rows, block), 1) % CAP).astype(F32)
        here = ranks == place
        pieces = [jnp.where(here, jnp.dot(gate_m[piece], spread, preferred_element_type=F32),
                            0.0).astype(BF16) for piece in range(2)]

        def mixed(values):
            values = values.reshape(block, width)
            return sum(jnp.dot(piece, values, preferred_element_type=F32) for piece in pieces)

        @pl.when(jnp.logical_not(within(p, wide_in)))
        def _():
            arrived(p, ret.at[0:2 * ny], ret.at[0:2 * ny - 2], r_recv, 1)
            acc[...] = acc[...] + mixed(ret[pl.ds(first, 2 * ny)])

        for f, q in enumerate(wide_in):
            @pl.when(p == q)
            def _():
                arrived(p, rwide.at[f], rwide.at[f, :, 0:2 * ny - 2], r_recv, 1)
                for xx in range(NX):
                    if f == 0:
                        twide[xx] = mixed(rwide[f, xx])
                    else:
                        twide[xx] = twide[xx] + mixed(rwide[f, xx])

    stages = {
        "slots": (slots_stage, nz), "near": (near_stage, nz), "far": (far_stage, nz),
        "core": (core_stage, nz), "shared": (shared_stage, 1), "routed": (routed_stage, nz),
        "sum1": (sum1_stage, nz + 1), "sum2": (sum2_stage, nz + 1), "sum3": (sum3_stage, nz + 1),
        "mix": (mix_stage, nz),
    }
    last = max(first + -(-stages[name][1] * den // num) for name, num, den, first in FLOW)
    acc[...] = jnp.zeros_like(acc)

    @pl.loop(0, last)
    def _(i):
        for name, num, den, first in FLOW:
            body, count = stages[name]

            def reached(steps):
                return jnp.minimum(num * jnp.maximum(steps, 0) // den, count)

            pl.loop(reached(i - first), reached(i + 1 - first))(body)

    out[...] = acc[...].astype(out.dtype)

    for p in range(nz):
        skip = 2 if p == zero else 0

        def sent(narrow, some, broad):
            if p in some:
                return broad.at[some.index(p), :, 0:2 * ny - skip]
            return narrow.at[0:2 * ny - skip]

        out_part, in_part = sent(xout, wide_out, xwide), sent(ret, wide_in, rwide)
        remote(out_part, out_part, a_send.at[p], a_recv.at[p], to_right).wait_send()
        remote(in_part, in_part, r_send.at[p], r_recv.at[p], to_right).wait_send()
        four = arr.at[:, 0, p]
        remote(four, four, c_send.at[p], c_recv.at[p], to_core).wait_send()
        if p not in wide_out:
            two, one = arr.at[0:2, 0, p], arr.at[0, 0, p]
            remote(two, two, x_send.at[p], xl_recv.at[p], to_right).wait_send()
            remote(one, one, h_send.at[p], hl_recv.at[p], to_right).wait_send()
    for j in range(nz + 1):
        remote(part.at[j], precv.at[j], p_send.at[j], p_recv.at[j], to_core).wait_send()
        if j not in wide_in:
            one, two = final.at[0, j], total.at[j, 0:2]
            remote(one, one, f_send.at[j], fl_recv.at[j], to_right).wait_send()
            remote(two, two, g_send.at[j], gl_recv.at[j], to_right).wait_send()


def layer(tokens, routes, gates, wg, wu, wd, sg, su, sd, nz):
    rows, width_all = tokens.shape
    routes, gates, sg, su = routes.T, gates.T, sg.T, su.T
    wg, wu = wg.transpose(0, 2, 1), wu.transpose(0, 2, 1)
    width = width_all // (2 * NX)
    ny = lax.axis_size("expert") // nz
    experts = 2 * nz * ny
    half = ny * CAP
    out_wide, in_wide = [max(len(part), 1) for part in plan_of(nz)[1:]]
    assert rows == 2 * half
    dma = pltpu.SemaphoreType.DMA
    vm = pltpu.VMEM
    scratch = [vm(a.shape, a.dtype) for a in (tokens, routes, gates, wg, wu, wd, sg, su, sd)]
    scratch += [
        vm((experts, rows), BF16),
        vm((rows, experts), BF16),
        vm((2, rows, experts), BF16),
        vm((experts, CAP, width), BF16),
        vm((out_wide, NX, 2 * ny, CAP, width), BF16),
        vm((NX, 2, nz, 2, half, width), BF16),
        vm((nz + 1, NX, 2, half, width), BF16),
        vm((nz + 1, NX, 2, half, width), BF16),
        vm((nz + 1, NX, 2, half, width), BF16),
        vm((2, nz + 1, half, width), BF16),
        vm((2, nz + 1, 2, half, width), BF16),
        vm((nz, 2, half, width), BF16),
        vm((experts, CAP, width), BF16),
        vm((in_wide, NX, 2 * ny, CAP, width), BF16),
        vm((NX, rows, width), F32),
        vm((rows, width), F32),
    ]
    scratch += [dma((9,)), dma((2,))]
    scratch += [dma((nz,)) for _ in range(10)]
    scratch += [dma((nz + 1,)) for _ in range(8)]
    scratch += [dma((nz,)) for _ in range(2)]
    return pl.pallas_call(
        functools.partial(kernel, nz, ny, routes.shape[0]),
        out_shape=jax.ShapeDtypeStruct((rows, width), BF16),
        in_specs=[pl.BlockSpec(memory_space=pl.ANY)] * 9,
        out_specs=pl.BlockSpec(memory_space=pltpu.VMEM),
        scratch_shapes=scratch,
        compiler_params=pltpu.CompilerParams(
            collective_id=0, has_side_effects=True, vmem_limit_bytes=60 * 1024 * 1024),
        cost_estimate=pl.CostEstimate(
            flops=7 * 10**9, bytes_accessed=12 * 10**6, transcendentals=10**6),
    )(tokens, routes, gates, wg, wu, wd, sg, su, sd)


def solution(mesh):
    nz = mesh.shape["expert"] // NY
    return jax.shard_map(
        functools.partial(layer, nz=nz),
        mesh=mesh,
        in_specs=(
            P("expert", None),
            P("expert", None),
            P("expert", None),
            P("expert", None, "seq"),
            P("expert", None, "seq"),
            P("expert", "seq", None),
            P(None, "seq"),
            P(None, "seq"),
            P("seq", None),
        ),
        out_specs=P("expert", "seq"),
        check_vma=False,
    )
```

```python
import functools
import jax
import jax.numpy as jnp
from jax import lax
from jax.experimental import pallas as pl
from jax.experimental.pallas import tpu as pltpu
from jax.sharding import PartitionSpec as P

MESH = pl.DeviceIdType.MESH
F32 = jnp.float32
BF16 = jnp.bfloat16
CAP = 32
NX = 4
NY = 4
EARLY = 8
PLAN = {8: ((-1, 0, 4, 2, -3, 3, -2, 1), (0, 1), (0, -1))}
FLOW = (
    ("shared", 1, 1, 1),
    ("mix", 1, 1, 12),
    ("near", 1, 1, 1),
    ("slots", 4, 1, 0),
    ("far", 1, 1, 2),
    ("core", 1, 1, 3),
    ("routed", 1, 1, 4),
    ("sum3", 1, 1, 8),
    ("sum1", 1, 1, 5),
    ("sum2", 1, 1, 6),
)


def plan_of(nz):
    default = [0] + [d for k in range(1, nz) for d in (k, -k)][:nz - 1]
    plan = PLAN.get(nz, (tuple(default), (0, 1), (0, -1)))
    return [[d % nz for d in part] for part in plan]


def dot_nt(a, b):
    return lax.dot_general(a, b, (((1,), (1,)), ((), ())), preferred_element_type=F32)


def kernel(nz, ny, top, tokens_h, routes_h, gates_h, wg_h, wu_h, wd_h, sg_h, su_h, sd_h, out,
           tokens, routes, gates, wg, wu, wd, sg, su, sd, rank_t, rank_m, gate_m, xout, xwide, arr, part, precv, total, thru, final,
           back, ret, rwide, twide, acc,
           w_sem, l_sem, a_send, a_recv, x_send, xl_recv, xr_recv, h_send, hl_recv, hr_recv,
           c_send, c_recv, p_send, p_recv, f_send, fl_recv, fr_recv, g_send, gl_recv, gr_recv,
           r_send, r_recv):
    rows = tokens.shape[0]
    width = xout.shape[2]
    half = ny * CAP
    experts = xout.shape[0]
    block = 2 * half
    seq, exp = lax.axis_index("seq"), lax.axis_index("expert")
    x, c = seq // 2, seq % 2
    z, y = exp // ny, exp % ny
    right, left, across = (x + 1) % NX, (x + NX - 1) % NX, (x + 2) % NX
    to_right = (right * 2 + c, exp)
    to_left = (left * 2 + c, exp)
    to_core = (x * 2 + 1 - c, exp)

    order, *whole = plan_of(nz)
    zero = order.index(0)
    wide_out, wide_in = [sorted(order.index(d) for d in part) for part in whole]

    def offset(p):
        value = 0
        for q, d in enumerate(order):
            value = jnp.where(p == q, d, value)
        return value

    def within(p, some):
        hit = p == nz + 1
        for q in some:
            hit = hit | (p == q)
        return hit

    def remote(src, dst, send, recv, target):
        return pltpu.make_async_remote_copy(
            src_ref=src, dst_ref=dst, send_sem=send, recv_sem=recv,
            device_id=target, device_id_type=MESH)

    small = [pltpu.make_async_copy(a, b, w_sem.at[6 + i]) for i, (a, b) in enumerate(
        ((routes_h, routes), (tokens_h, tokens), (gates_h, gates)))]
    for copy in small:
        copy.start()

    barrier = pltpu.get_barrier_semaphore()

    @pl.loop(1, nz * ny)
    def _(d):
        pl.semaphore_signal(barrier, inc=1, device_id=(seq, (exp + d) % (nz * ny)),
                            device_id_type=MESH)

    for target in (to_right, to_left, to_core):
        pl.semaphore_signal(barrier, inc=1, device_id=target, device_id_type=MESH)

    loads = [pltpu.make_async_copy(a, b, w_sem.at[i]) for i, (a, b) in enumerate(
        ((sg_h, sg), (su_h, su), (sd_h, sd), (wg_h, wg), (wu_h, wu), (wd_h, wd)))]
    small[0].wait()

    eid = lax.broadcasted_iota(jnp.int32, (experts, rows), 0)
    chosen = jnp.zeros((experts, rows), F32)
    for k in range(top):
        chosen = chosen + jnp.where(routes[k:k + 1, :] == eid, 1.0, 0.0)
    row = lax.broadcasted_iota(jnp.int32, (rows, rows), 0)
    col = lax.broadcasted_iota(jnp.int32, (rows, rows), 1)
    before = jnp.where(row < col, 1.0, 0.0).astype(BF16)
    rank = jnp.dot(chosen.astype(BF16), before, preferred_element_type=F32)
    rank_t[...] = jnp.where(chosen > 0.5, rank, -1.0).astype(BF16)

    def send_one(src, dst, p, dy, send, recv, target, local):
        copy = remote(src, dst, send.at[p], recv.at[p], target)
        if dy:
            copy.start()
        else:
            @pl.when(p != zero)
            def _():
                copy.start()

            @pl.when(p == zero)
            def _():
                pltpu.make_async_copy(src, dst, l_sem.at[local]).start()

    def fill_slots(p):
        zb = (z + offset(p)) % nz
        first = zb * (2 * ny)
        row = lax.broadcasted_iota(jnp.int32, (block, experts), 0)
        col = lax.broadcasted_iota(jnp.int32, (block, experts), 1)
        spread = jnp.where(row // CAP + first == col, 1.0, 0.0).astype(BF16)
        ranks = jnp.dot(spread, rank_t[...], preferred_element_type=F32)
        place = (lax.broadcasted_iota(jnp.int32, (block, rows), 0) % CAP).astype(F32)
        pick = jnp.where(ranks == place, 1.0, 0.0).astype(BF16)

        def gathered(s):
            mine = tokens[:, pl.ds(pl.multiple_of(s * width, width), width)]
            slots = jnp.dot(pick, mine, preferred_element_type=F32).astype(BF16)
            return slots.reshape(2 * ny, CAP, width)

        @pl.when(jnp.logical_not(within(p, wide_out)))
        def _():
            xout[pl.ds(first, 2 * ny)] = gathered(seq)

        for f, q in enumerate(wide_out):
            @pl.when(p == q)
            def _():
                for xx in range(NX):
                    xwide[f, xx] = gathered(2 * xx + c)

    def slots_stage(p):
        zb = (z + offset(p)) % nz

        @pl.when(p >= EARLY)
        def _():
            fill_slots(p)

        @pl.when(jnp.logical_not(within(p, wide_out)))
        def _():
            for dy in range(ny):
                there = zb * ny + (y + dy) % ny
                send_one(xout.at[pl.ds(2 * there, 2)],
                         arr.at[x, c, p, :, dy * CAP:(dy + 1) * CAP, :],
                         p, dy, a_send, a_recv, (seq, there), 0)

        for f, q in enumerate(wide_out):
            @pl.when(p == q)
            def _():
                for dy in range(ny):
                    yy = (y + dy) % ny
                    send_one(xwide.at[f, :, pl.ds(2 * yy, 2)],
                             arr.at[:, c, p, :, dy * CAP:(dy + 1) * CAP, :],
                             p, dy, a_send, a_recv, (seq, zb * ny + yy), 0)

    small[1].wait()
    for copy in loads:
        copy.start()
    pl.loop(0, min(EARLY, nz))(fill_slots)
    pl.semaphore_wait(barrier, nz * ny - 1 + 3)

    def arrived(p, all_of, rest_of, recv, local):
        @pl.when(p != zero)
        def _():
            remote(all_of, all_of, a_send.at[p], recv.at[p], to_right).wait_recv()

        @pl.when(p == zero)
        def _():
            first = all_of.at[(slice(None),) * (len(all_of.shape) - 3)
                              + ((slice(None), slice(0, CAP)) if local == 0 else (slice(0, 2),))]
            pltpu.make_async_copy(first, first, l_sem.at[local]).wait()
            remote(rest_of, rest_of, a_send.at[p], recv.at[p], to_right).wait_recv()

    def near_stage(p):
        @pl.when(within(p, wide_out))
        def _():
            own = arr.at[:, c, p]
            arrived(p, own, arr.at[:, c, p, :, CAP:half, :], a_recv, 0)
            remote(own, own, c_send.at[p], c_recv.at[p], to_core).start()

        @pl.when(jnp.logical_not(within(p, wide_out)))
        def _():
            own = arr.at[x, c, p]
            arrived(p, own, arr.at[x, c, p, :, CAP:half, :], a_recv, 0)
            remote(own, own, x_send.at[p], xl_recv.at[p], to_right).start()
            remote(own, own, x_send.at[p], xr_recv.at[p], to_left).start()
            remote(own, own, c_send.at[p], c_recv.at[p], to_core).start()

    def far_stage(p):
        @pl.when(jnp.logical_not(within(p, wide_out)))
        def _():
            from_left, from_right = arr.at[left, c, p], arr.at[right, c, p]
            remote(from_left, from_left, x_send.at[p], xl_recv.at[p], to_right).wait_recv()
            remote(from_left.at[0], from_left.at[0], h_send.at[p], hl_recv.at[p], to_right).start()
            remote(from_left, from_left, c_send.at[p], c_recv.at[p], to_core).start()
            remote(from_right, from_right, x_send.at[p], xr_recv.at[p], to_left).wait_recv()
            remote(from_right.at[1], from_right.at[1], h_send.at[p], hr_recv.at[p], to_left).start()
            remote(from_right, from_right, c_send.at[p], c_recv.at[p], to_core).start()

    def core_stage(p):
        @pl.when(jnp.logical_not(within(p, wide_out)))
        def _():
            far = arr.at[across, c, p]
            remote(far.at[0], far.at[0], h_send.at[p], hl_recv.at[p], to_right).wait_recv()
            remote(far.at[1], far.at[1], h_send.at[p], hr_recv.at[p], to_left).wait_recv()
            remote(far, far, c_send.at[p], c_recv.at[p], to_core).start()

    def send_part(j):
        remote(part.at[j], precv.at[j], p_send.at[j], p_recv.at[j], to_core).start()

    def down(hidden, weights):
        for parity, dst in ((1 - c, part), (c, total)):
            for xx in range(NX):
                cols = pl.ds(pl.multiple_of((2 * xx + parity) * width, width), width)
                value = jnp.dot(hidden, weights(cols), preferred_element_type=F32).astype(BF16)
                yield dst, xx, value

    def turn_tables():
        small[2].wait()
        eid = lax.broadcasted_iota(jnp.int32, (experts, rows), 0)
        weight = jnp.zeros((experts, rows), F32)
        for k in range(top):
            weight = weight + jnp.where(routes[k:k + 1, :] == eid, gates[k:k + 1, :], 0.0)
        row = lax.broadcasted_iota(jnp.int32, (rows, rows), 0)
        col = lax.broadcasted_iota(jnp.int32, (rows, rows), 1)
        same = jnp.where(row == col, 1.0, 0.0).astype(BF16)
        high = weight.astype(BF16)
        low = (weight - high.astype(F32)).astype(BF16)
        rank_m[...] = dot_nt(same, rank_t[...]).astype(BF16)
        gate_m[0] = dot_nt(same, high).astype(BF16)
        gate_m[1] = dot_nt(same, low).astype(BF16)

    def shared_stage(_):
        turn_tables()
        for copy in loads[:3]:
            copy.wait()
        gate = dot_nt(tokens[...], sg[...])
        up = dot_nt(tokens[...], su[...])
        hidden = (gate / (1.0 + jnp.exp(-gate)) * up).astype(BF16)
        for dst, xx, value in down(hidden, lambda cols: sd[:, cols]):
            dst[nz, xx] = value.reshape(2, half, width)
        send_part(nz)

    def routed_stage(p):
        @pl.when(p == 0)
        def _():
            for copy in loads[3:]:
                copy.wait()

        other = arr.at[:, 1 - c, p]
        remote(other, other, c_send.at[p], c_recv.at[p], to_core).wait_recv()
        for e in range(2):
            gate = jnp.zeros((half, wg.shape[1]), F32)
            up = jnp.zeros((half, wg.shape[1]), F32)
            for s in range(2 * NX):
                a = arr[s // 2, s % 2, p, e]
                gate = gate + dot_nt(a, wg[e, :, s * width:(s + 1) * width])
                up = up + dot_nt(a, wu[e, :, s * width:(s + 1) * width])
            hidden = (gate / (1.0 + jnp.exp(-gate)) * up).astype(BF16)
            for dst, xx, value in down(hidden, lambda cols: wd[e, :, cols]):
                dst[p, xx, e] = value
        send_part(p)

    def sum1_stage(j):
        remote(part.at[j], precv.at[j], p_send.at[j], p_recv.at[j], to_core).wait_recv()

        def add(xx):
            value = total[j, xx].astype(F32) + precv[j, xx].astype(F32)
            if not wide_in:
                total[j, xx] = value.astype(BF16)
                return

            @pl.when(j < nz)
            def _():
                total[j, xx] = value.astype(BF16)

            @pl.when(j == nz)
            def _():
                total[j, xx] = (value + twide[xx].reshape(2, half, width)).astype(BF16)

        @pl.when(jnp.logical_not(within(j, wide_in)))
        def _():
            add(across)
            remote(total.at[j, across, 0], thru.at[0, j], f_send.at[j], fl_recv.at[j], to_right).start()
            remote(total.at[j, across, 1], thru.at[1, j], f_send.at[j], fr_recv.at[j], to_left).start()
            add(right)
            remote(total.at[j, right, 1], final.at[0, j, 1], g_send.at[j], gl_recv.at[j], to_right).start()
            add(left)
            remote(total.at[j, left, 0], final.at[1, j, 0], g_send.at[j], gr_recv.at[j], to_left).start()
            add(x)

        for f, q in enumerate(wide_in):
            @pl.when(j == q)
            def _():
                for xx in range(NX):
                    total[q, xx] = (total[q, xx].astype(F32) + precv[q, xx].astype(F32)).astype(BF16)
                zb = (z + nz - order[q]) % nz
                for dy in range(ny):
                    there = zb * ny + (y + ny - dy) % ny
                    send_one(total.at[q, :, :, dy * CAP:(dy + 1) * CAP, :],
                             rwide.at[f, :, pl.ds(2 * y, 2)],
                             j, dy, r_send, r_recv, (seq, there), 1)

    def sum2_stage(j):
        @pl.when(jnp.logical_not(within(j, wide_in)))
        def _():
            remote(thru.at[0, j], thru.at[0, j], f_send.at[j], fl_recv.at[j], to_right).wait_recv()
            total[j, right, 0] = (total[j, right, 0].astype(F32) + thru[0, j].astype(F32)).astype(BF16)
            remote(total.at[j, right, 0], final.at[0, j, 0], g_send.at[j], gl_recv.at[j], to_right).start()
            remote(thru.at[1, j], thru.at[1, j], f_send.at[j], fr_recv.at[j], to_left).wait_recv()
            total[j, left, 1] = (total[j, left, 1].astype(F32) + thru[1, j].astype(F32)).astype(BF16)
            remote(total.at[j, left, 1], final.at[1, j, 1], g_send.at[j], gr_recv.at[j], to_left).start()

    def sum3_stage(j):
        @pl.when(jnp.logical_not(within(j, wide_in)))
        def _():
            remote(final.at[0, j], final.at[0, j], g_send.at[j], gl_recv.at[j], to_right).wait_recv()
            remote(final.at[1, j], final.at[1, j], g_send.at[j], gr_recv.at[j], to_left).wait_recv()
            value = total[j, x].astype(F32) + final[0, j].astype(F32) + final[1, j].astype(F32)

            @pl.when(j == nz)
            def _():
                acc[...] = acc[...] + value.reshape(rows, width)

            @pl.when(j < nz)
            def _():
                back[j] = value.astype(BF16)
                zb = (z + nz - offset(j)) % nz
                for dy in range(ny):
                    there = zb * ny + (y + ny - dy) % ny
                    send_one(back.at[j, :, dy * CAP:(dy + 1) * CAP, :], ret.at[pl.ds(2 * exp, 2)],
                             j, dy, r_send, r_recv, (seq, there), 1)

    def mix_stage(p):
        zb = (z + offset(p)) % nz
        first = zb * (2 * ny)

        row = lax.broadcasted_iota(jnp.int32, (experts, block), 0)
        col = lax.broadcasted_iota(jnp.int32, (experts, block), 1)
        spread = jnp.where(col // CAP + first == row, 1.0, 0.0).astype(BF16)
        ranks = jnp.dot(rank_m[...], spread, preferred_element_type=F32)
        place = (lax.broadcasted_iota(jnp.int32, (rows, block), 1) % CAP).astype(F32)
        here = ranks == place
        pieces = [jnp.where(here, jnp.dot(gate_m[piece], spread, preferred_element_type=F32),
                            0.0).astype(BF16) for piece in range(2)]

        def mixed(values):
            values = values.reshape(block, width)
            return sum(jnp.dot(piece, values, preferred_element_type=F32) for piece in pieces)

        @pl.when(jnp.logical_not(within(p, wide_in)))
        def _():
            arrived(p, ret.at[0:2 * ny], ret.at[0:2 * ny - 2], r_recv, 1)
            acc[...] = acc[...] + mixed(ret[pl.ds(first, 2 * ny)])

        for f, q in enumerate(wide_in):
            @pl.when(p == q)
            def _():
                arrived(p, rwide.at[f], rwide.at[f, :, 0:2 * ny - 2], r_recv, 1)
                for xx in range(NX):
                    if f == 0:
                        twide[xx] = mixed(rwide[f, xx])
                    else:
                        twide[xx] = twide[xx] + mixed(rwide[f, xx])

    stages = {
        "slots": (slots_stage, nz), "near": (near_stage, nz), "far": (far_stage, nz),
        "core": (core_stage, nz), "shared": (shared_stage, 1), "routed": (routed_stage, nz),
        "sum1": (sum1_stage, nz + 1), "sum2": (sum2_stage, nz + 1), "sum3": (sum3_stage, nz + 1),
        "mix": (mix_stage, nz),
    }
    last = max(first + -(-stages[name][1] * den // num) for name, num, den, first in FLOW)
    acc[...] = jnp.zeros_like(acc)

    @pl.loop(0, last)
    def _(i):
        for name, num, den, first in FLOW:
            body, count = stages[name]

            def reached(steps):
                return jnp.minimum(num * jnp.maximum(steps, 0) // den, count)

            pl.loop(reached(i - first), reached(i + 1 - first))(body)

    out[...] = acc[...].astype(out.dtype)

    for p in range(nz):
        skip = 2 if p == zero else 0

        def sent(narrow, some, broad):
            if p in some:
                return broad.at[some.index(p), :, 0:2 * ny - skip]
            return narrow.at[0:2 * ny - skip]

        out_part, in_part = sent(xout, wide_out, xwide), sent(ret, wide_in, rwide)
        remote(out_part, out_part, a_send.at[p], a_recv.at[p], to_right).wait_send()
        remote(in_part, in_part, r_send.at[p], r_recv.at[p], to_right).wait_send()
        four = arr.at[:, 0, p]
        remote(four, four, c_send.at[p], c_recv.at[p], to_core).wait_send()
        if p not in wide_out:
            two, one = arr.at[0:2, 0, p], arr.at[0, 0, p]
            remote(two, two, x_send.at[p], xl_recv.at[p], to_right).wait_send()
            remote(one, one, h_send.at[p], hl_recv.at[p], to_right).wait_send()
    for j in range(nz + 1):
        remote(part.at[j], precv.at[j], p_send.at[j], p_recv.at[j], to_core).wait_send()
        if j not in wide_in:
            one, two = final.at[0, j], total.at[j, 0:2]
            remote(one, one, f_send.at[j], fl_recv.at[j], to_right).wait_send()
            remote(two, two, g_send.at[j], gl_recv.at[j], to_right).wait_send()


def layer(tokens, routes, gates, wg, wu, wd, sg, su, sd, nz):
    rows, width_all = tokens.shape
    routes, gates, sg, su = routes.T, gates.T, sg.T, su.T
    wg, wu = wg.transpose(0, 2, 1), wu.transpose(0, 2, 1)
    width = width_all // (2 * NX)
    ny = lax.axis_size("expert") // nz
    experts = 2 * nz * ny
    half = ny * CAP
    out_wide, in_wide = [max(len(part), 1) for part in plan_of(nz)[1:]]
    assert rows == 2 * half
    dma = pltpu.SemaphoreType.DMA
    vm = pltpu.VMEM
    scratch = [vm(a.shape, a.dtype) for a in (tokens, routes, gates, wg, wu, wd, sg, su, sd)]
    scratch += [
        vm((experts, rows), BF16),
        vm((rows, experts), BF16),
        vm((2, rows, experts), BF16),
        vm((experts, CAP, width), BF16),
        vm((out_wide, NX, 2 * ny, CAP, width), BF16),
        vm((NX, 2, nz, 2, half, width), BF16),
        vm((nz + 1, NX, 2, half, width), BF16),
        vm((nz + 1, NX, 2, half, width), BF16),
        vm((nz + 1, NX, 2, half, width), BF16),
        vm((2, nz + 1, half, width), BF16),
        vm((2, nz + 1, 2, half, width), BF16),
        vm((nz, 2, half, width), BF16),
        vm((experts, CAP, width), BF16),
        vm((in_wide, NX, 2 * ny, CAP, width), BF16),
        vm((NX, rows, width), F32),
        vm((rows, width), F32),
    ]
    scratch += [dma((9,)), dma((2,))]
    scratch += [dma((nz,)) for _ in range(10)]
    scratch += [dma((nz + 1,)) for _ in range(8)]
    scratch += [dma((nz,)) for _ in range(2)]
    return pl.pallas_call(
        functools.partial(kernel, nz, ny, routes.shape[0]),
        out_shape=jax.ShapeDtypeStruct((rows, width), BF16),
        in_specs=[pl.BlockSpec(memory_space=pl.ANY)] * 9,
        out_specs=pl.BlockSpec(memory_space=pltpu.VMEM),
        scratch_shapes=scratch,
        compiler_params=pltpu.CompilerParams(
            collective_id=0, has_side_effects=True, vmem_limit_bytes=60 * 1024 * 1024),
        cost_estimate=pl.CostEstimate(
            flops=7 * 10**9, bytes_accessed=12 * 10**6, transcendentals=10**6),
    )(tokens, routes, gates, wg, wu, wd, sg, su, sd)


def solution(mesh):
    nz = mesh.shape["expert"] // NY
    return jax.shard_map(
        functools.partial(layer, nz=nz),
        mesh=mesh,
        in_specs=(
            P("expert", None),
            P("expert", None),
            P("expert", None),
            P("expert", None, "seq"),
            P("expert", None, "seq"),
            P("expert", "seq", None),
            P(None, "seq"),
            P(None, "seq"),
            P("seq", None),
        ),
        out_specs=P("expert", "seq"),
        check_vma=False,
    )
```
